32 devices in a mesh: member: 2 (over y), space: 8 (over z, x), tracer: 2 (over core).
Axes of the slice: x: 2, y: 2, z: 4, core: 2. Of those that a mesh axis runs over, the one named last changes fastest.
Arguments:
- lam_new: float32 [48, 4, 64, 512], P(('member', 'tracer'), None, 'space'), parts along dimension 0, may hold values from -6 to 6
- tracers: float32 [48, 4, 64, 512], P(('member', 'tracer'), None, 'space'), parts along dimension 0, may hold values from -6 to 6
- velocity_u: float32 [8, 64, 512], P('member', 'space'), parts along dimension 0, may hold values from -3 to 3
- velocity_v: float32 [8, 64, 512], P('member', 'space'), parts along dimension 0, may hold values from -3 to 3
- diffusivity: float32 [8, 64, 512], P('member', 'space'), parts along dimension 0, may hold values from 0.05 to 0.3
- light: float32 [8, 64, 512], P('member', 'space'), parts along dimension 0, may hold values from 0.25 to 2
- land_sea: int32 [4, 64, 512], P(None, 'space'), may hold values 0 or 1
- partner: int32 [64], P('space'), may hold values from 0 to 63, as said below
- decay: float32 [24], P('tracer'), may hold values from 0.05 to 0.5
- w_in: float32 [8, 24], replicated, may hold values from -1.25 to 1.25
- w_out: float32 [24, 8], replicated, may hold values from -2 to 2
Outputs:
- lam_old: float32 [48, 4, 64, 512], P(('member', 'tracer'), None, 'space'), parts along dimension 0
The draws below stay inside these ranges and needn't reach their ends.
There are 2 independent parts, one for each index of `member`. The reference program is written for one: setup_inputs(seed, part) draws one part's arguments, and reference() takes and returns one part's arrays. A program takes and returns all parts, laid end to end along the dimension named above; an argument that names none is the same for every part. Nothing has to cross between parts.
Inputs may be any that keep to these rules, and one draw needn't show every extreme that they name: partner[partner[i]] == i, and partner[i] lies in the mirrored block of 8 columns: partner[i] // 8 == 7 - i // 8.
All inputs are finite; a program needn't handle non-finite values. No bound on the sum of `land_sea` on one device may be relied on, other than what follows from the above.
Results may differ from the reference program's by a relative error of at most 0.00013.
Values sent between devices are 32-bit elements; how exact they have to be, the bound alone decides.
No kernel may reach another device: no remote copies, remote signals or barrier semaphores. Data moves between devices by JAX's collectives and lax.ppermute only.
A program may use at most 128 MiB of HBM per device.

```python
import math
import jax
import jax.numpy as jnp
from jax import lax

NTR = 24
H = 8
K = 4
CI = 8
NJ = 512
NI = 64


def draw_partner(key, part):
    blocks = NI // CI
    half_blocks = blocks // 2
    keys = jax.random.split(key, half_blocks)
    perms = jax.vmap(lambda sub_key: jax.random.permutation(sub_key, CI))(keys).astype(jnp.int32)
    inverse = jnp.argsort(perms, axis=1, stable=True).astype(jnp.int32)
    low_index = jnp.arange(half_blocks, dtype=jnp.int32)
    low_part = (blocks - 1 - low_index)[:, None] * CI + perms
    high_part = low_index[::-1][:, None] * CI + inverse[::-1]
    return jnp.concatenate([low_part, high_part], axis=0).reshape(-1).astype(jnp.int32)


def with_ends(values, stream_key, least, high):
    place = [jax.random.randint(jax.random.fold_in(stream_key, axis), (), 0, length) for axis, length in enumerate(values.shape)]
    longest = values.shape.index(max(values.shape))
    neighbour = place[:longest] + [(place[longest] + 1) % values.shape[longest]] + place[longest + 1:]
    return values.at[tuple(place)].set(least).at[tuple(neighbour)].set(high)


def steps_of(rng, dims, pieces, least, high):
    level, own = 1.0, jax.random.fold_in(rng, 6)
    for axis_at, parts in pieces:
        draws = jnp.exp(jax.random.uniform(jax.random.fold_in(own, axis_at), (parts,), jnp.float32, least / len(pieces), high / len(pieces)))
        level = level * jnp.repeat(draws, dims[axis_at] // parts).reshape([-1 if axis == axis_at else 1 for axis in range(len(dims))])
    return level


def bell_draw(key, dims, width, limit, cuts=(), kind=jnp.bfloat16):
    entries = jax.random.normal(key, dims, jnp.float32) * width
    if len(cuts) > 0:
        entries = steps_of(key, dims, cuts, -0.22, 0.18) * entries
    return jnp.clip(entries, min=-limit, max=limit).astype(kind)


def setup_inputs(seed: int = 0, part: int = 0) -> dict:
    seeds = jax.random.split(jax.random.key(seed), 12)
    part_keys = jax.random.split(jax.random.fold_in(seeds[11], part), 12)
    lam_new = bell_draw(part_keys[0], (NTR, K, NI, NJ), 1.0, 6.0, ((0, 2), (2, 8)), jnp.float32)
    tracers = bell_draw(part_keys[1], (NTR, K, NI, NJ), 1.0, 6.0, ((0, 2), (2, 8)), jnp.float32)
    velocity_u = bell_draw(part_keys[2], (K, NI, NJ), 0.5, 3.0, ((1, 8),), jnp.float32)
    velocity_v = bell_draw(part_keys[3], (K, NI, NJ), 0.5, 3.0, ((1, 8),), jnp.float32)
    diffusivity = jnp.clip(jnp.exp(math.log(0.3) - 1.7917595 * jax.random.uniform(part_keys[4], (K, NI, NJ), jnp.float32) ** steps_of(part_keys[4], (K, NI, NJ), ((1, 8),), -0.2, 0.2)), 0.05, 0.3)
    light = jnp.clip(0.25 + 1.75 * jax.random.uniform(part_keys[5], (K, NI, NJ), jnp.float32) ** steps_of(part_keys[5], (K, NI, NJ), ((1, 8),), -0.2, 0.2), 0.25, 2.0)
    land_sea = with_ends((jax.random.randint(seeds[6], (K, NI, NJ), 0, 4) < 3).astype(jnp.int32), jax.random.fold_in(seeds[6], 1), 0, 1)
    partner = draw_partner(jax.random.fold_in(seeds[11], 71), part)
    decay = jnp.clip(jnp.exp(math.log(0.5) - 2.3025851 * jax.random.uniform(seeds[8], (NTR,), jnp.float32) ** steps_of(seeds[8], (NTR,), ((0, 2),), -0.2, 0.2)), 0.05, 0.5)
    w_in = bell_draw(seeds[9], (H, NTR), NTR ** -0.5, 1.25, (), jnp.float32)
    w_out = bell_draw(seeds[10], (NTR, H), H ** -0.5, 2.0, (), jnp.float32)
    return {"lam_new": lam_new, "tracers": tracers, "velocity_u": velocity_u, "velocity_v": velocity_v, "diffusivity": diffusivity, "light": light, "land_sea": land_sea, "partner": partner, "decay": decay, "w_in": w_in, "w_out": w_out}


def advance(state, velocity_u, velocity_v, diffusivity, light, sea_mask, partner, decay, w_in, w_out):
    highest = lax.Precision.HIGHEST
    east_state = jnp.roll(state, -1, axis=2)
    m_east = sea_mask * jnp.roll(sea_mask, -1, axis=1)
    u_east = 0.5 * (velocity_u + jnp.roll(velocity_u, -1, axis=1))
    k_east = 0.5 * (diffusivity + jnp.roll(diffusivity, -1, axis=1))
    flux_east = m_east * (u_east * 0.5 * (state + east_state) - k_east * (east_state - state))
    tendency = -(flux_east - jnp.roll(flux_east, 1, axis=2))
    m_north = sea_mask[..., :-1] * sea_mask[..., 1:]
    v_north = 0.5 * (velocity_v[..., :-1] + velocity_v[..., 1:])
    k_north = 0.5 * (diffusivity[..., :-1] + diffusivity[..., 1:])
    lower_rows = state[..., :-1]
    upper_rows = state[..., 1:]
    flux_north = m_north * (v_north * 0.5 * (lower_rows + upper_rows) - k_north * (upper_rows - lower_rows))
    top_rows = state[..., -1]
    partner_rows = jnp.take(top_rows, partner, axis=2)
    mask_top = sea_mask[..., -1]
    m_fold = mask_top * jnp.take(mask_top, partner, axis=1)
    v_top = velocity_v[..., -1]
    k_top = diffusivity[..., -1]
    v_fold = 0.5 * (v_top - jnp.take(v_top, partner, axis=1))
    k_fold = 0.5 * (k_top + jnp.take(k_top, partner, axis=1))
    flux_fold = m_fold * (v_fold * 0.5 * (top_rows + partner_rows) - k_fold * (partner_rows - top_rows))
    outward = jnp.concatenate([flux_north, flux_fold[..., None]], axis=-1)
    inward = jnp.concatenate([jnp.zeros_like(flux_fold)[..., None], flux_north], axis=-1)
    tendency = tendency - (outward - inward)
    uptake = jnp.einsum('ha,akij->hkij', w_in, state, precision=highest)
    reaction = jnp.einsum('bh,hkij->bkij', w_out, light[None] * jnp.tanh(uptake), precision=highest)
    source = -decay[:, None, None, None] * state + reaction
    return sea_mask[None] * (state + tendency + source)

def reference(lam_new, tracers, velocity_u, velocity_v, diffusivity, light, land_sea, partner, decay, w_in, w_out):
    sea_mask = land_sea.astype(jnp.float32)

    def forward(state):
        return advance(state, velocity_u, velocity_v, diffusivity, light, sea_mask, partner, decay, w_in, w_out)
    result, pullback = jax.vjp(forward, tracers)
    return pullback(lam_new)[0]
```

```python
import functools

import jax
import jax.numpy as jnp
from jax import lax
from jax.experimental import pallas as pl
from jax.experimental.pallas import tpu as pltpu
from jax.sharding import PartitionSpec as P

F32 = jnp.float32
VMEM = pl.BlockSpec(memory_space=pltpu.VMEM)
SMEM = pl.BlockSpec(memory_space=pltpu.SMEM)


def sums_kernel(w_in, w_out, lam, tracers, vel_u, vel_v, kappa, sea_int, sums, pack_even, pack_odd):
    count, levels, cols, rows = lam.shape
    reactions = w_in.shape[0]
    first = lax.axis_index("tracer") * count
    even = lax.rem(lax.axis_index("space"), 2) == 0
    edge = count * levels

    for target, is_east in ((pack_even, even), (pack_odd, jnp.logical_not(even))):
        line = pl.ds(jnp.where(is_east, cols - 1, 0), 1)
        sign = jnp.where(is_east, -0.5, 0.5)
        for a in range(count):
            for k in range(levels):
                target[pl.ds(a * levels + k, 1), :] = lam[a, k, line, :]
        for k in range(levels):
            target[pl.ds(edge + k, 1), :] = 0.25 * vel_u[k, line, :] + sign * kappa[k, line, :]
            target[pl.ds(edge + levels + k, 1), :] = sea_int[k, line, :].astype(F32)

    lane = lax.broadcasted_iota(jnp.int32, (cols, 128), 1)
    top = jnp.zeros((cols, 128), F32)
    last = rows - 128
    for a in range(count):
        for k in range(levels):
            top = jnp.where(lane == a * levels + k, lam[a, k, :, last:][:, 127:], top)
    for k in range(levels):
        coef = 0.5 * kappa[k, :, last:] - 0.25 * vel_v[k, :, last:]
        top = jnp.where(lane == edge + k, coef[:, 127:], top)
        top = jnp.where(lane == edge + levels + k, sea_int[k, :, last:].astype(F32)[:, 127:], top)
    pack_odd[pl.ds(edge + 2 * levels, cols), :128] = top

    def level(k, carry):
        for field, weight, base in ((tracers, lambda h, a: w_in[h, first + a], 0), (lam, lambda h, a: w_out[h, first + a], reactions)):
            total = [None] * reactions
            for a in range(count):
                x = field[a, k]
                for h in range(reactions):
                    term = weight(h, a) * x
                    total[h] = term if a == 0 else total[h] + term
            for h in range(reactions):
                sums[base + h, k] = total[h]
        return carry

    lax.fori_loop(0, levels, level, 0)


def final_kernel(w_in, decay, partner, lam, vel_u, vel_v, kappa, light, sea_int, sums, sums_other, from_even, from_odd, from_fold, out, fold_rows, halo_e, halo_w):
    count, levels, cols, rows = lam.shape
    reactions = w_in.shape[0]
    first = lax.axis_index("tracer") * count
    place, strips = lax.axis_index("space"), lax.axis_size("space")
    even = lax.rem(place, 2) == 0
    edge = count * levels
    at = edge + 2 * levels
    neighbour = jnp.where(even, lax.rem(place + strips - 1, strips), lax.rem(place + 1, strips))
    folded = neighbour == strips - 1 - place
    fold = jnp.where(folded, from_odd[pl.ds(at, cols), :128], from_fold[...])
    halo_e[...] = jnp.where(even, from_even[...], from_odd[pl.ds(0, at), :])
    halo_w[...] = jnp.where(even, from_odd[pl.ds(0, at), :], from_even[...])
    sub = lax.broadcasted_iota(jnp.int32, (cols, 128), 0)
    turned = jnp.zeros((cols, 128), F32)
    for i in range(cols):
        pick = lax.rem(partner[i], cols)
        row = jnp.sum(jnp.where(sub == pick, fold, 0.0), axis=0, keepdims=True)
        turned = jnp.where(sub == i, row, turned)
    fold_rows[...] = turned

    col = lax.broadcasted_iota(jnp.int32, (cols, rows), 0)
    row = lax.broadcasted_iota(jnp.int32, (cols, rows), 1)
    is_east, is_west = col == cols - 1, col == 0
    is_top, is_bottom = row == rows - 1, row == 0
    lane = lax.broadcasted_iota(jnp.int32, (cols, 128), 1)

    def halo(ref, index):
        return ref[pl.ds(index, 1), :]

    def folded_at(index):
        return jnp.sum(jnp.where(lane == index, fold_rows[...], 0.0), axis=1, keepdims=True)

    def level(k, carry):
        sea = sea_int[k].astype(F32)
        u, v, kap = vel_u[k], vel_v[k], kappa[k]
        p, q = 0.25 * u + 0.5 * kap, 0.25 * u - 0.5 * kap
        pn, qn = 0.25 * v + 0.5 * kap, 0.25 * v - 0.5 * kap

        def eastern(x, index):
            return jnp.where(is_east, halo(halo_e, index), pltpu.roll(x, cols - 1, 0))

        def western(x, index):
            return jnp.where(is_west, halo(halo_w, index), pltpu.roll(x, 1, 0))

        def northern(x, index):
            return jnp.where(is_top, folded_at(index), pltpu.roll(x, rows - 1, 1))

        c_e = sea * eastern(sea, edge + levels + k) * (p + eastern(p, edge + k))
        c_w = sea * western(sea, edge + levels + k) * (western(q, edge + k) + q)
        c_n = sea * northern(sea, edge + levels + k) * (pn + northern(pn, edge + k))
        c_s = jnp.where(is_bottom, 0.0, sea * pltpu.roll(sea, 1, 1) * (pltpu.roll(qn, 1, 1) + qn))
        own = sea + (c_w + c_s - c_e - c_n)
        lit = light[k] * sea
        gain = []
        for h in range(reactions):
            t = jnp.tanh(sums[h, k] + sums_other[h, k])
            gain.append(lit * (1.0 - t * t) * (sums[reactions + h, k] + sums_other[reactions + h, k]))
        for a in range(count):
            x = lam[a, k]
            y = (own - decay[a] * sea) * x
            y += c_e * eastern(x, a * levels + k)
            y -= c_w * western(x, a * levels + k)
            y += c_n * northern(x, a * levels + k)
            y -= c_s * pltpu.roll(x, 1, 1)
            for h in range(reactions):
                y += w_in[h, first + a] * gain[h]
            out[a, k] = y
        return carry

    lax.fori_loop(0, levels, level, 0)


def body(lam, tracers, vel_u, vel_v, kappa, light, sea_int, partner, decay, w_in, w_out):
    count, levels, cols, rows = lam.shape
    reactions = w_in.shape[0]
    edge = (count + 2) * levels
    n = lax.axis_size("space")
    sums, pack_even, pack_odd = pl.pallas_call(
        sums_kernel,
        name="sums",
        out_shape=(
            jax.ShapeDtypeStruct((2 * reactions, levels, cols, rows), F32),
            jax.ShapeDtypeStruct((edge, rows), F32),
            jax.ShapeDtypeStruct((edge + cols, rows), F32),
        ),
        in_specs=[SMEM, SMEM] + [VMEM] * 6,
        out_specs=(VMEM, VMEM, VMEM),
        compiler_params=pltpu.CompilerParams(vmem_limit_bytes=32 << 20),
    )(w_in, w_out.T, lam, tracers, vel_u, vel_v, kappa, sea_int)
    even_pairs = [(s, s ^ 1) for s in range(n)]
    odd_pairs = [(s, (s + 1) % n if s % 2 else (s - 1) % n) for s in range(n)]
    fold_pairs = [(s, n - 1 - s) for s in range(n) if (s, n - 1 - s) not in odd_pairs]
    top = pack_odd[edge:, :128]
    sums_other = lax.ppermute(sums, "tracer", [(0, 1), (1, 0)])
    from_odd = lax.ppermute(pack_odd, "space", odd_pairs)
    from_even = lax.ppermute(pack_even, "space", even_pairs)
    from_fold = lax.ppermute(top, "space", fold_pairs)
    return pl.pallas_call(
        final_kernel,
        name="final",
        out_shape=jax.ShapeDtypeStruct(lam.shape, F32),
        in_specs=[SMEM] * 3 + [VMEM] * 11,
        out_specs=VMEM,
        scratch_shapes=[
            pltpu.VMEM((cols, 128), F32),
            pltpu.VMEM((edge, rows), F32),
            pltpu.VMEM((edge, rows), F32),
        ],
        compiler_params=pltpu.CompilerParams(vmem_limit_bytes=32 << 20),
    )(w_in, decay, partner, lam, vel_u, vel_v, kappa, light, sea_int, sums, sums_other, from_even, from_odd, from_fold)


def solution(mesh):
    placed = (
        P(("member", "tracer"), None, "space", None),
        P(("member", "tracer"), None, "space", None),
        P("member", "space", None),
        P("member", "space", None),
        P("member", "space", None),
        P("member", "space", None),
        P(None, "space", None),
        P("space"),
        P("tracer"),
        P(),
        P(),
    )
    return jax.shard_map(
        body,
        mesh=mesh,
        in_specs=placed,
        out_specs=P(("member", "tracer"), None, "space", None),
        check_vma=False,
    )
```

```python
import jax
import jax.numpy as jnp
from jax import lax
from jax.experimental import pallas as pl
from jax.experimental.pallas import tpu as pltpu
from jax.sharding import PartitionSpec as P

F32 = jnp.float32
VMEM = pl.BlockSpec(memory_space=pltpu.VMEM)
SMEM = pl.BlockSpec(memory_space=pltpu.SMEM)
HBM = pl.BlockSpec(memory_space=pltpu.HBM)
LANES = 128


def pack_kernel(
    vel_u_hbm, vel_v_hbm, kappa_hbm, sea_hbm, lam_hbm, tracers_hbm, light_hbm, w_in_hbm, w_out_hbm, decay_hbm, partner_hbm,
    vel_u, vel_v, kappa, sea, lam, tracers, light, w_in, w_out, decay, partner, pack_east, pack_west, top_out, sems,
):
    count, levels, cols, rows = lam.shape
    edge = count * levels
    tall = edge + 2 * levels
    sources = (vel_u_hbm, vel_v_hbm, kappa_hbm, sea_hbm, lam_hbm, tracers_hbm, light_hbm, w_in_hbm, w_out_hbm, decay_hbm, partner_hbm)
    targets = (vel_u, vel_v, kappa, sea, lam, tracers, light, w_in, w_out, decay, partner)
    copies = [pltpu.make_async_copy(s, t, sems.at[i]) for i, (s, t) in enumerate(zip(sources, targets))]
    for copy in copies:
        copy.start()
    for copy in copies[:5]:
        copy.wait()

    for target, line, sign in ((pack_east, slice(cols - 1, cols), -0.5), (pack_west, slice(0, 1), 0.5)):

        def put(index, value):
            for c in range(rows // LANES):
                target[pl.ds(c * tall + index, 1), :] = value[:, c * LANES : (c + 1) * LANES]

        for a in range(count):
            for k in range(levels):
                put(a * levels + k, lam[a, k, line, :])
        for k in range(levels):
            put(edge + k, 0.25 * vel_u[k, line, :] + sign * kappa[k, line, :])
            put(edge + levels + k, sea[k, line, :].astype(F32))

    lane = lax.broadcasted_iota(jnp.int32, (cols, LANES), 1)
    top = jnp.zeros((cols, LANES), F32)
    last = rows - LANES

    def placed(top, index, value):
        return jnp.where(lane == index, pltpu.roll(value, index + 1, 1), top)

    for a in range(count):
        for k in range(levels):
            top = placed(top, a * levels + k, lam[a, k, :, last:])
    for k in range(levels):
        top = placed(top, edge + k, 0.5 * kappa[k, :, last:] - 0.25 * vel_v[k, :, last:])
        top = placed(top, edge + levels + k, sea[k, :, last:].astype(F32))
    for target in (pack_east, pack_west):
        target[pl.ds(rows // LANES * tall, cols), :] = top
    top_out[...] = top
    for copy in copies[5:]:
        copy.wait()


def sums_kernel(w_in, w_out, lam, tracers, sums):
    count, levels, cols, rows = lam.shape
    reactions = w_in.shape[0]
    first = lax.axis_index("tracer") * count

    def level(k, carry):
        for field, weight, base in ((tracers, w_in, 0), (lam, w_out, reactions)):
            total = [None] * reactions
            for a in range(count):
                x = field[a, k]
                for h in range(reactions):
                    term = weight[h, first + a] * x
                    total[h] = term if a == 0 else total[h] + term
            for h in range(reactions):
                sums[base + h, k] = total[h]
        return carry

    lax.fori_loop(0, levels, level, 0)


def inner_kernel(decay, lam, vel_u, vel_v, kappa, sea_int, out):
    count, levels, cols, rows = lam.shape
    col = lax.broadcasted_iota(jnp.int32, (cols, rows), 0)
    row = lax.broadcasted_iota(jnp.int32, (cols, rows), 1)

    def level(k, carry):
        sea = sea_int[k].astype(F32)
        u, v, kap = 0.25 * vel_u[k], 0.25 * vel_v[k], 0.5 * kappa[k]
        east = jnp.where(col == cols - 1, 0.0, sea * pltpu.roll(sea, cols - 1, 0))
        north = jnp.where(row == rows - 1, 0.0, sea * pltpu.roll(sea, rows - 1, 1))
        p, q = u + kap, u - kap
        pn, qn = v + kap, v - kap
        c_e = east * (p + pltpu.roll(p, cols - 1, 0))
        c_w = pltpu.roll(east * (q + pltpu.roll(q, cols - 1, 0)), 1, 0)
        c_n = north * (pn + pltpu.roll(pn, rows - 1, 1))
        c_s = pltpu.roll(north * (qn + pltpu.roll(qn, rows - 1, 1)), 1, 1)
        own = sea + (c_w + c_s - c_e - c_n)
        for a in range(count):
            x = lam[a, k]
            y = (own - decay[a] * sea) * x
            y += c_e * pltpu.roll(x, cols - 1, 0)
            y -= c_w * pltpu.roll(x, 1, 0)
            y += c_n * pltpu.roll(x, rows - 1, 1)
            y -= c_s * pltpu.roll(x, 1, 1)
            out[a, k] = y
        return carry

    lax.fori_loop(0, levels, level, 0)


def react_kernel(w_in, light, sea, sums, sums_other, inner, out):
    count, levels, cols, rows = inner.shape
    reactions = w_in.shape[0]
    first = lax.axis_index("tracer") * count

    def level(k, carry):
        lit = light[k] * sea[k].astype(F32)
        gain = []
        for h in range(reactions):
            t = jnp.tanh(sums[h, k] + sums_other[h, k])
            gain.append(lit * (1.0 - t * t) * (sums[reactions + h, k] + sums_other[reactions + h, k]))
        for a in range(count):
            y = inner[a, k]
            for h in range(reactions):
                y += w_in[h, first + a] * gain[h]
            out[a, k] = y
        return carry

    lax.fori_loop(0, levels, level, 0)


def edges_kernel(
    partner, lam, vel_u, vel_v, kappa, sea_int, inner, from_west, from_east, from_fold, out_hbm,
    out, turned, sems,
):
    count, levels, cols, rows = lam.shape
    edge = count * levels
    tall = edge + 2 * levels
    chunks = rows // LANES
    place, strips = lax.axis_index("space"), lax.axis_size("space")
    to_east, to_west = lax.rem(place + 1, strips), lax.rem(place + strips - 1, strips)
    mirror = strips - 1 - place
    for i in range(cols):
        pick = lax.rem(partner[i], cols)
        across = from_fold[pl.ds(pick, 1), :]
        across = jnp.where(mirror == to_east, from_east[pl.ds(chunks * tall + pick, 1), :], across)
        across = jnp.where(mirror == to_west, from_west[pl.ds(chunks * tall + pick, 1), :], across)
        turned[pl.ds(i, 1), :] = across
    sub = lax.broadcasted_iota(jnp.int32, (cols, LANES), 0)
    lane = lax.broadcasted_iota(jnp.int32, (cols, LANES), 1)
    side = jnp.where(sub == 0, -1.0, jnp.where(sub == cols - 1, 1.0, 0.0))
    across = turned[...]

    def beyond(c, index):
        at = pl.ds(c * tall + index, 1)
        return jnp.where(sub == 0, from_west[at, :], from_east[at, :])

    def folded_at(index):
        return pltpu.roll(across, LANES - 1 - index, 1)

    def copy(k):
        return pltpu.make_async_copy(out.at[:, k], out_hbm.at[:, k], sems.at[k])

    for k in range(levels):
        for c in range(chunks):
            part = slice(c * LANES, (c + 1) * LANES)
            sea, u, kap = sea_int[k, :, part].astype(F32), 0.25 * vel_u[k, :, part], 0.5 * kappa[k, :, part]
            mine = jnp.where(sub == 0, u - kap, u + kap)
            coef = side * sea * beyond(c, edge + levels + k) * (mine + beyond(c, edge + k))
            if c == chunks - 1:
                up = 0.25 * vel_v[k, :, part] + kap + folded_at(edge + k)
                fold = jnp.where(lane == LANES - 1, sea * folded_at(edge + levels + k) * up, 0.0)
            for a in range(count):
                x = lam[a, k, :, part]
                y = inner[a, k, :, part] + coef * (beyond(c, a * levels + k) - x)
                if c == chunks - 1:
                    y += fold * (folded_at(a * levels + k) - x)
                out[a, k, :, part] = y
        copy(k).start()
    for k in range(levels):
        copy(k).wait()


def cost(flops, count):
    return pl.CostEstimate(flops=0, bytes_accessed=0, transcendentals=0)


def body(lam, tracers, vel_u, vel_v, kappa, light, sea_int, partner, decay, w_in, w_out):
    count, levels, cols, rows = lam.shape
    reactions = w_in.shape[0]
    tall = (count + 2) * levels * (rows // LANES)
    n = lax.axis_size("space")
    params = pltpu.CompilerParams(vmem_limit_bytes=32 << 20)
    whole = jax.ShapeDtypeStruct(lam.shape, F32)
    shares = jax.ShapeDtypeStruct((2 * reactions, levels, cols, rows), F32)
    tile = jax.ShapeDtypeStruct((cols, LANES), F32)
    arguments = (vel_u, vel_v, kappa, sea_int, lam, tracers, light, w_in, w_out.T, decay, partner)
    vel_u, vel_v, kappa, sea_int, lam, tracers, light, w_in, w_out, decay, partner, pack_east, pack_west, top = pl.pallas_call(
        pack_kernel,
        name="pack",
        out_shape=(
            *(jax.ShapeDtypeStruct(x.shape, x.dtype) for x in arguments),
            jax.ShapeDtypeStruct((tall + cols, LANES), F32),
            jax.ShapeDtypeStruct((tall + cols, LANES), F32),
            tile,
        ),
        in_specs=[HBM] * 11,
        out_specs=(VMEM,) * 14,
        scratch_shapes=[pltpu.SemaphoreType.DMA((11,))],
        compiler_params=params,
        cost_estimate=cost(0, 4 * lam.size),
    )(*(pltpu.with_memory_space_constraint(x, pltpu.HBM) for x in arguments))
    eastward = [(s, (s + 1) % n) for s in range(n)]
    westward = [(s, (s - 1) % n) for s in range(n)]
    mirrored = [(s, n - 1 - s) for s in range(n)]
    from_fold = lax.ppermute(top, "space", [p for p in mirrored if p not in eastward + westward])
    from_east = lax.ppermute(pack_west, "space", westward)
    from_west = lax.ppermute(pack_east, "space", eastward)
    sums = pl.pallas_call(
        sums_kernel,
        name="sums",
        out_shape=shares,
        in_specs=[SMEM] * 2 + [VMEM] * 2,
        out_specs=VMEM,
        compiler_params=params,
        cost_estimate=cost(32 * lam.size, 4 * lam.size),
    )(w_in, w_out, lam, tracers)
    sums_other = lax.ppermute(sums, "tracer", [(0, 1), (1, 0)])
    inner = pl.pallas_call(
        inner_kernel,
        name="inner",
        out_shape=whole,
        in_specs=[SMEM] + [VMEM] * 5,
        out_specs=VMEM,
        compiler_params=params,
        cost_estimate=cost(10 * lam.size, 4 * lam.size),
    )(decay, lam, vel_u, vel_v, kappa, sea_int)
    inner = pl.pallas_call(
        react_kernel,
        name="react",
        out_shape=whole,
        in_specs=[SMEM] + [VMEM] * 5,
        out_specs=VMEM,
        compiler_params=params,
        cost_estimate=cost(16 * lam.size, 4 * lam.size),
    )(w_in, light, sea_int, sums, sums_other, inner)
    return pl.pallas_call(
        edges_kernel,
        name="edges",
        out_shape=whole,
        in_specs=[SMEM] + [VMEM] * 9,
        out_specs=HBM,
        scratch_shapes=[
            pltpu.VMEM(lam.shape, F32),
            pltpu.VMEM((cols, LANES), F32),
            pltpu.SemaphoreType.DMA((levels,)),
        ],
        compiler_params=params,
        cost_estimate=cost(10 * lam.size, 4 * lam.size),
    )(partner, lam, vel_u, vel_v, kappa, sea_int, inner, from_west, from_east, from_fold)


def solution(mesh):
    placed = (
        P(("member", "tracer"), None, "space", None),
        P(("member", "tracer"), None, "space", None),
        P("member", "space", None),
        P("member", "space", None),
        P("member", "space", None),
        P("member", "space", None),
        P(None, "space", None),
        P("space"),
        P("tracer"),
        P(),
        P(),
    )
    return jax.shard_map(
        body,
        mesh=mesh,
        in_specs=placed,
        out_specs=P(("member", "tracer"), None, "space", None),
        check_vma=False,
    )
```

```python
import jax
import jax.numpy as jnp
from jax import lax
from jax.experimental import pallas as pl
from jax.experimental.pallas import tpu as pltpu
from jax.sharding import PartitionSpec as P

F32, BF16 = jnp.float32, jnp.bfloat16
VMEM = pl.BlockSpec(memory_space=pltpu.VMEM)
SMEM = pl.BlockSpec(memory_space=pltpu.SMEM)
HBM = pl.BlockSpec(memory_space=pltpu.HBM)
LANES = 128


def halves(x):
    high = x.astype(BF16)
    return high, (x - high.astype(F32)).astype(BF16)


def spread(target, weight, blocks, width, cols):
    lane = lax.broadcasted_iota(jnp.int32, (cols, width * cols), 1)
    sub = lax.broadcasted_iota(jnp.int32, (cols, width * cols), 0)
    square, diagonal = lane // cols, lane % cols == sub
    chosen = [square == other for other in range(width)]
    high, low = [], []
    for block in range(blocks):
        row = jnp.zeros((cols, width * cols), F32)
        for other in range(width):
            row = jnp.where(chosen[other], weight(block, other), row)
        row = jnp.where(diagonal, row, 0.0)
        top = row.astype(BF16).astype(F32)
        high.append(top)
        low.append(row - top)
    target[...] = jnp.concatenate(high + low, axis=0).astype(BF16)


def product(matrix, x):
    half = matrix.shape[0] // 2
    high, low = halves(x)
    first = jnp.dot(matrix[...], high, preferred_element_type=F32)
    return first[:half] + first[half:] + jnp.dot(matrix[:half], low, preferred_element_type=F32)


def pack_kernel(
    w_in_hbm, w_out_hbm, decay_hbm, partner_hbm, vel_u_hbm, vel_v_hbm, kappa_hbm, sea_hbm, lam_hbm, tracers_hbm, light_hbm,
    vel_u, vel_v, kappa, sea, lam, tracers, light, pack_east, pack_west, top_out, to_uptake, to_weighted, to_tracers, fade, order,
    w_in, w_out, decay, partner, sems,
):
    count, levels, cols, rows = lam.shape
    edge = count * levels
    tall = edge + 2 * levels
    reactions = w_in.shape[0]
    sources = (w_in_hbm, w_out_hbm, decay_hbm, partner_hbm, vel_u_hbm, vel_v_hbm, kappa_hbm, sea_hbm, lam_hbm, tracers_hbm, light_hbm)
    targets = (w_in, w_out, decay, partner, vel_u, vel_v, kappa, sea, lam, tracers, light)
    copies = [pltpu.make_async_copy(s, t, sems.at[i]) for i, (s, t) in enumerate(zip(sources, targets))]
    for copy in copies:
        copy.start()
    first = lax.axis_index("tracer") * count
    for copy in copies[:4]:
        copy.wait()
    for a in range(count):
        fade[pl.ds(a, 1), :] = jnp.full((1, rows), decay[a], F32)
    sub = lax.broadcasted_iota(jnp.int32, (cols, LANES), 0)
    picks = jnp.zeros((cols, LANES), jnp.int32)
    for i in range(cols):
        picks = jnp.where(sub == i, lax.rem(partner[i], cols), picks)
    order[...] = picks
    spread(to_uptake, lambda h, a: w_in[h, first + a], reactions, count, cols)
    spread(to_weighted, lambda h, a: w_out[h, first + a], reactions, count, cols)
    spread(to_tracers, lambda a, h: w_in[h, first + a], count, reactions, cols)
    for copy in copies[4:9]:
        copy.wait()

    for target, line, sign in ((pack_east, slice(cols - 1, cols), -0.5), (pack_west, slice(0, 1), 0.5)):

        def put(index, value):
            for c in range(rows // LANES):
                target[pl.ds(c * tall + index, 1), :] = value[:, c * LANES : (c + 1) * LANES]

        for a in range(count):
            for k in range(levels):
                put(a * levels + k, lam[a, k, line, :])
        for k in range(levels):
            put(edge + k, 0.25 * vel_u[k, line, :] + sign * kappa[k, line, :])
            put(edge + levels + k, sea[k, line, :].astype(F32))

    lane = lax.broadcasted_iota(jnp.int32, (cols, LANES), 1)
    top = jnp.zeros((cols, LANES), F32)
    last = rows - LANES

    def placed(top, index, value):
        return jnp.where(lane == index, pltpu.roll(value, index + 1, 1), top)

    for a in range(count):
        for k in range(levels):
            top = placed(top, a * levels + k, lam[a, k, :, last:])
    for k in range(levels):
        top = placed(top, edge + k, 0.5 * kappa[k, :, last:] - 0.25 * vel_v[k, :, last:])
        top = placed(top, edge + levels + k, sea[k, :, last:].astype(F32))
    for target in (pack_east, pack_west):
        target[pl.ds(rows // LANES * tall, cols), :] = top
    top_out[...] = top
    for copy in copies[9:]:
        copy.wait()


def sums_kernel(to_uptake, to_weighted, lam, tracers, sums):
    count, levels, cols, rows = lam.shape
    reactions = sums.shape[0] // 2
    for k in range(levels):
        for field, matrix, base in ((tracers, to_uptake, 0), (lam, to_weighted, reactions)):
            total = product(matrix, field[:, k].reshape(count * cols, rows))
            sums[pl.ds(base, reactions), k] = total.reshape(reactions, cols, rows)


def inner_kernel(fade, lam, vel_u, vel_v, kappa, sea_int, top, out, top_out):
    count, levels, cols, rows = lam.shape
    col = lax.broadcasted_iota(jnp.int32, (cols, rows), 0)
    row = lax.broadcasted_iota(jnp.int32, (cols, rows), 1)

    def level(k, carry):
        sea = sea_int[k].astype(F32)
        u, v, kap = 0.25 * vel_u[k], 0.25 * vel_v[k], 0.5 * kappa[k]
        east = jnp.where(col == cols - 1, 0.0, sea * pltpu.roll(sea, cols - 1, 0))
        north = jnp.where(row == rows - 1, 0.0, sea * pltpu.roll(sea, rows - 1, 1))
        p, q = u + kap, u - kap
        pn, qn = v + kap, v - kap
        c_e = east * (p + pltpu.roll(p, cols - 1, 0))
        c_w = pltpu.roll(east * (q + pltpu.roll(q, cols - 1, 0)), 1, 0)
        c_n = north * (pn + pltpu.roll(pn, rows - 1, 1))
        c_s = pltpu.roll(north * (qn + pltpu.roll(qn, rows - 1, 1)), 1, 1)
        own = sea + (c_w + c_s - c_e - c_n)
        for a in range(count):
            x = lam[a, k]
            y = (own - fade[pl.ds(a, 1), :] * sea) * x
            y += c_e * pltpu.roll(x, cols - 1, 0)
            y -= c_w * pltpu.roll(x, 1, 0)
            y += c_n * pltpu.roll(x, rows - 1, 1)
            y -= c_s * pltpu.roll(x, 1, 1)
            out[a, k] = y
        return carry

    top_out[...] = top[...]
    lax.fori_loop(0, levels, level, 0)


def react_kernel(to_tracers, light, sea, sums, sums_other, inner, out):
    count, levels, cols, rows = inner.shape
    reactions = sums.shape[0] // 2
    for k in range(levels):
        lit = light[k] * sea[k].astype(F32)
        gain = []
        for h in range(reactions):
            t = jnp.tanh(sums[h, k] + sums_other[h, k])
            gain.append(lit * (1.0 - t * t) * (sums[reactions + h, k] + sums_other[reactions + h, k]))
        coupled = product(to_tracers, jnp.concatenate(gain, axis=0))
        out[:, k] = inner[:, k] + coupled.reshape(count, cols, rows)


def edges_kernel(
    order, lam, vel_u, vel_v, kappa, sea_int, inner, from_west, from_east, from_fold, out_hbm,
    out, sems,
):
    count, levels, cols, rows = lam.shape
    edge = count * levels
    tall = edge + 2 * levels
    chunks = rows // LANES
    place, strips = lax.axis_index("space"), lax.axis_size("space")
    to_east, to_west = lax.rem(place + 1, strips), lax.rem(place + strips - 1, strips)
    mirror = strips - 1 - place
    at_fold = pl.ds(chunks * tall, cols)
    fold_rows = jnp.where(mirror == to_east, from_east[at_fold, :], from_fold[...])
    fold_rows = jnp.where(mirror == to_west, from_west[at_fold, :], fold_rows)
    across = jnp.zeros((cols, LANES), F32)
    for p in range(cols):
        across = jnp.where(order[...] == p, fold_rows[p : p + 1, :], across)
    sub = lax.broadcasted_iota(jnp.int32, (cols, LANES), 0)
    lane = lax.broadcasted_iota(jnp.int32, (cols, LANES), 1)
    side = jnp.where(sub == 0, -1.0, jnp.where(sub == cols - 1, 1.0, 0.0))

    def beyond(c, index):
        at = pl.ds(c * tall + index, 1)
        return jnp.where(sub == 0, from_west[at, :], from_east[at, :])

    def folded_at(index):
        return pltpu.roll(across, LANES - 1 - index, 1)

    def copy(k):
        return pltpu.make_async_copy(out.at[:, k], out_hbm.at[:, k], sems.at[k])

    def level(k, carry):
        for c in range(chunks):
            part = slice(c * LANES, (c + 1) * LANES)
            sea, u, kap = sea_int[k, :, part].astype(F32), 0.25 * vel_u[k, :, part], 0.5 * kappa[k, :, part]
            mine = jnp.where(sub == 0, u - kap, u + kap)
            coef = side * sea * beyond(c, edge + levels + k) * (mine + beyond(c, edge + k))
            if c == chunks - 1:
                up = 0.25 * vel_v[k, :, part] + kap + folded_at(edge + k)
                fold = jnp.where(lane == LANES - 1, sea * folded_at(edge + levels + k) * up, 0.0)
            for a in range(count):
                x = lam[a, k, :, part]
                y = inner[a, k, :, part] + coef * (beyond(c, a * levels + k) - x)
                if c == chunks - 1:
                    y += fold * (folded_at(a * levels + k) - x)
                out[a, k, :, part] = y
        copy(k).start()
        return carry

    lax.fori_loop(0, levels, level, 0)
    for k in range(levels):
        copy(k).wait()


def cost(flops, count):
    return pl.CostEstimate(flops=0, bytes_accessed=0, transcendentals=0)


def body(lam, tracers, vel_u, vel_v, kappa, light, sea_int, partner, decay, w_in, w_out):
    count, levels, cols, rows = lam.shape
    reactions = w_in.shape[0]
    tall = (count + 2) * levels * (rows // LANES)
    n = lax.axis_size("space")
    params = pltpu.CompilerParams(vmem_limit_bytes=32 << 20)
    whole = jax.ShapeDtypeStruct(lam.shape, F32)
    shares = jax.ShapeDtypeStruct((2 * reactions, levels, cols, rows), F32)
    tile = jax.ShapeDtypeStruct((cols, LANES), F32)
    scalars = (w_in, w_out.T, decay, partner)
    arguments = (vel_u, vel_v, kappa, sea_int, lam, tracers, light)
    vel_u, vel_v, kappa, sea_int, lam, tracers, light, pack_east, pack_west, top, to_uptake, to_weighted, to_tracers, fade, order = pl.pallas_call(
        pack_kernel,
        name="pack",
        out_shape=(
            *(jax.ShapeDtypeStruct(x.shape, x.dtype) for x in arguments),
            jax.ShapeDtypeStruct((tall + cols, LANES), F32),
            jax.ShapeDtypeStruct((tall + cols, LANES), F32),
            tile,
            *[jax.ShapeDtypeStruct((2 * reactions * cols, count * cols), BF16)] * 2,
            jax.ShapeDtypeStruct((2 * count * cols, reactions * cols), BF16),
            jax.ShapeDtypeStruct((count, rows), F32),
            jax.ShapeDtypeStruct((cols, LANES), jnp.int32),
        ),
        in_specs=[HBM] * 11,
        out_specs=(VMEM,) * 15,
        scratch_shapes=[*(pltpu.SMEM(x.shape, x.dtype) for x in scalars), pltpu.SemaphoreType.DMA((11,))],
        compiler_params=params,
        cost_estimate=cost(0, 4 * lam.size),
    )(*(pltpu.with_memory_space_constraint(x, pltpu.HBM) for x in scalars + arguments))
    eastward = [(s, (s + 1) % n) for s in range(n)]
    westward = [(s, (s - 1) % n) for s in range(n)]
    mirrored = [(s, n - 1 - s) for s in range(n)]
    from_east = lax.ppermute(pack_west, "space", westward)
    from_west = lax.ppermute(pack_east, "space", eastward)
    sums = pl.pallas_call(
        sums_kernel,
        name="sums",
        out_shape=shares,
        in_specs=[VMEM] * 4,
        out_specs=VMEM,
        compiler_params=params,
        cost_estimate=cost(32 * lam.size, 4 * lam.size),
    )(to_uptake, to_weighted, lam, tracers)
    sums_other = lax.ppermute(sums, "tracer", [(0, 1), (1, 0)])
    inner, top = pl.pallas_call(
        inner_kernel,
        name="inner",
        out_shape=(whole, tile),
        in_specs=[VMEM] * 7,
        out_specs=(VMEM, VMEM),
        compiler_params=params,
        cost_estimate=cost(10 * lam.size, 4 * lam.size),
    )(fade, lam, vel_u, vel_v, kappa, sea_int, top)
    from_fold = lax.ppermute(top, "space", [p for p in mirrored if p not in eastward + westward])
    inner = pl.pallas_call(
        react_kernel,
        name="react",
        out_shape=whole,
        in_specs=[VMEM] * 6,
        out_specs=VMEM,
        compiler_params=params,
        cost_estimate=cost(16 * lam.size, 4 * lam.size),
    )(to_tracers, light, sea_int, sums, sums_other, inner)
    return pl.pallas_call(
        edges_kernel,
        name="edges",
        out_shape=whole,
        in_specs=[VMEM] * 10,
        out_specs=HBM,
        scratch_shapes=[
            pltpu.VMEM(lam.shape, F32),
            pltpu.SemaphoreType.DMA((levels,)),
        ],
        compiler_params=params,
        cost_estimate=cost(10 * lam.size, 4 * lam.size),
    )(order, lam, vel_u, vel_v, kappa, sea_int, inner, from_west, from_east, from_fold)


def solution(mesh):
    placed = (
        P(("member", "tracer"), None, "space", None),
        P(("member", "tracer"), None, "space", None),
        P("member", "space", None),
        P("member", "space", None),
        P("member", "space", None),
        P("member", "space", None),
        P(None, "space", None),
        P("space"),
        P("tracer"),
        P(),
        P(),
    )
    return jax.shard_map(
        body,
        mesh=mesh,
        in_specs=placed,
        out_specs=P(("member", "tracer"), None, "space", None),
        check_vma=False,
    )
```

```python
import jax
import jax.numpy as jnp
from jax import lax
from jax.experimental import pallas as pl
from jax.experimental.pallas import tpu as pltpu
from jax.sharding import PartitionSpec as P

F32, BF16 = jnp.float32, jnp.bfloat16
VMEM = pl.BlockSpec(memory_space=pltpu.VMEM)
SMEM = pl.BlockSpec(memory_space=pltpu.SMEM)
HBM = pl.BlockSpec(memory_space=pltpu.HBM)
LANES = 128


def halves(x):
    high = x.astype(BF16)
    return high, (x - high.astype(F32)).astype(BF16)


def spread(target, weight, blocks, width, cols):
    lane = lax.broadcasted_iota(jnp.int32, (cols, width * cols), 1)
    sub = lax.broadcasted_iota(jnp.int32, (cols, width * cols), 0)
    square, diagonal = lane // cols, lane % cols == sub
    chosen = [square == other for other in range(width)]
    high, low = [], []
    for block in range(blocks):
        row = jnp.zeros((cols, width * cols), F32)
        for other in range(width):
            row = jnp.where(chosen[other], weight(block, other), row)
        row = jnp.where(diagonal, row, 0.0)
        top = row.astype(BF16).astype(F32)
        high.append(top)
        low.append(row - top)
    target[...] = jnp.concatenate(high + low, axis=0).astype(BF16)


def product(matrix, x):
    half = matrix.shape[0] // 2
    high, low = halves(x)
    first = jnp.dot(matrix[...], high, preferred_element_type=F32)
    return first[:half] + first[half:] + jnp.dot(matrix[:half], low, preferred_element_type=F32)


def pack_kernel(
    w_in_hbm, w_out_hbm, decay_hbm, partner_hbm, vel_u_hbm, vel_v_hbm, kappa_hbm, sea_hbm, lam_hbm, tracers_hbm, light_hbm,
    vel_u, vel_v, kappa, sea, light, both, pack_east, pack_west, top_out, to_uptake, to_weighted, to_uptake_other, to_weighted_other, to_tracers, fade, order,
    w_in, w_out, decay, partner, sems,
):
    lam, tracers = both.at[0], both.at[1]
    count, levels, cols, rows = lam.shape
    edge = count * levels
    tall = edge + 2 * levels
    reactions = w_in.shape[0]
    sources = (w_in_hbm, w_out_hbm, decay_hbm, partner_hbm, vel_u_hbm, vel_v_hbm, kappa_hbm, sea_hbm, lam_hbm, tracers_hbm, light_hbm)
    targets = (w_in, w_out, decay, partner, vel_u, vel_v, kappa, sea, lam, tracers, light)
    copies = [pltpu.make_async_copy(s, t, sems.at[i]) for i, (s, t) in enumerate(zip(sources, targets))]
    for copy in copies:
        copy.start()
    first = lax.axis_index("tracer") * count
    for copy in copies[:4]:
        copy.wait()
    for a in range(count):
        fade[pl.ds(a, 1), :] = jnp.full((1, rows), decay[a], F32)
    sub = lax.broadcasted_iota(jnp.int32, (cols, LANES), 0)
    picks = jnp.zeros((cols, LANES), jnp.int32)
    for i in range(cols):
        picks = jnp.where(sub == i, lax.rem(partner[i], cols), picks)
    order[...] = picks
    spread(to_uptake, lambda h, a: w_in[h, first + a], reactions, count, cols)
    spread(to_weighted, lambda h, a: w_out[h, first + a], reactions, count, cols)
    second = count - first
    spread(to_uptake_other, lambda h, a: w_in[h, second + a], reactions, count, cols)
    spread(to_weighted_other, lambda h, a: w_out[h, second + a], reactions, count, cols)
    spread(to_tracers, lambda a, h: w_in[h, first + a], count, reactions, cols)
    for copy in copies[4:9]:
        copy.wait()

    for target, line, sign in ((pack_east, slice(cols - 1, cols), -0.5), (pack_west, slice(0, 1), 0.5)):

        def put(index, value):
            for c in range(rows // LANES):
                target[pl.ds(c * tall + index, 1), :] = value[:, c * LANES : (c + 1) * LANES]

        for a in range(count):
            for k in range(levels):
                put(a * levels + k, lam[a, k, line, :])
        for k in range(levels):
            put(edge + k, 0.25 * vel_u[k, line, :] + sign * kappa[k, line, :])
            put(edge + levels + k, sea[k, line, :].astype(F32))

    lane = lax.broadcasted_iota(jnp.int32, (cols, LANES), 1)
    top = jnp.zeros((cols, LANES), F32)
    last = rows - LANES

    def placed(top, index, value):
        return jnp.where(lane == index, pltpu.roll(value, index + 1, 1), top)

    for a in range(count):
        for k in range(levels):
            top = placed(top, a * levels + k, lam[a, k, :, last:])
    for k in range(levels):
        top = placed(top, edge + k, 0.5 * kappa[k, :, last:] - 0.25 * vel_v[k, :, last:])
        top = placed(top, edge + levels + k, sea[k, :, last:].astype(F32))
    for target in (pack_east, pack_west):
        target[pl.ds(rows // LANES * tall, cols), :] = top
    top_out[...] = top
    for copy in copies[9:]:
        copy.wait()


def sums_kernel(to_uptake, to_weighted, both, sums):
    _, count, levels, cols, rows = both.shape
    reactions = sums.shape[0] // 2
    for k in range(levels):
        for field, matrix, base in ((1, to_uptake, 0), (0, to_weighted, reactions)):
            total = product(matrix, both[field, :, k].reshape(count * cols, rows))
            sums[pl.ds(base, reactions), k] = total.reshape(reactions, cols, rows)


def inner_kernel(fade, both, vel_u, vel_v, kappa, sea_int, out):
    lam = both.at[0]
    count, levels, cols, rows = lam.shape
    col = lax.broadcasted_iota(jnp.int32, (cols, rows), 0)
    row = lax.broadcasted_iota(jnp.int32, (cols, rows), 1)

    def level(k, carry):
        sea = sea_int[k].astype(F32)
        u, v, kap = 0.25 * vel_u[k], 0.25 * vel_v[k], 0.5 * kappa[k]
        east = jnp.where(col == cols - 1, 0.0, sea * pltpu.roll(sea, cols - 1, 0))
        north = jnp.where(row == rows - 1, 0.0, sea * pltpu.roll(sea, rows - 1, 1))
        p, q = u + kap, u - kap
        pn, qn = v + kap, v - kap
        c_e = east * (p + pltpu.roll(p, cols - 1, 0))
        c_w = pltpu.roll(east * (q + pltpu.roll(q, cols - 1, 0)), 1, 0)
        c_n = north * (pn + pltpu.roll(pn, rows - 1, 1))
        c_s = pltpu.roll(north * (qn + pltpu.roll(qn, rows - 1, 1)), 1, 1)
        own = sea + (c_w + c_s - c_e - c_n)
        for a in range(count):
            x = lam[a, k]
            y = (own - fade[pl.ds(a, 1), :] * sea) * x
            y += c_e * pltpu.roll(x, cols - 1, 0)
            y -= c_w * pltpu.roll(x, 1, 0)
            y += c_n * pltpu.roll(x, rows - 1, 1)
            y -= c_s * pltpu.roll(x, 1, 1)
            out[a, k] = y
        return carry

    lax.fori_loop(0, levels, level, 0)


def react_kernel(to_uptake, to_weighted, to_tracers, light, sea, sums, both, inner, out):
    count, levels, cols, rows = inner.shape
    reactions = sums.shape[0] // 2
    for k in range(levels):
        lit = light[k] * sea[k].astype(F32)
        uptake = product(to_uptake, both[1, :, k].reshape(count * cols, rows))
        weighted = product(to_weighted, both[0, :, k].reshape(count * cols, rows))
        gain = []
        for h in range(reactions):
            part = slice(h * cols, (h + 1) * cols)
            t = jnp.tanh(sums[h, k] + uptake[part])
            gain.append(lit * (1.0 - t * t) * (sums[reactions + h, k] + weighted[part]))
        coupled = product(to_tracers, jnp.concatenate(gain, axis=0))
        out[:, k] = inner[:, k] + coupled.reshape(count, cols, rows)


def edges_kernel(
    order, both, vel_u, vel_v, kappa, sea_int, inner, from_west, from_east, from_fold, out_hbm,
    out, sems,
):
    lam = both.at[0]
    count, levels, cols, rows = lam.shape
    edge = count * levels
    tall = edge + 2 * levels
    chunks = rows // LANES
    place, strips = lax.axis_index("space"), lax.axis_size("space")
    to_east, to_west = lax.rem(place + 1, strips), lax.rem(place + strips - 1, strips)
    mirror = strips - 1 - place
    at_fold = pl.ds(chunks * tall, cols)
    fold_rows = jnp.where(mirror == to_east, from_east[at_fold, :], from_fold[...])
    fold_rows = jnp.where(mirror == to_west, from_west[at_fold, :], fold_rows)
    across = jnp.zeros((cols, LANES), F32)
    for p in range(cols):
        across = jnp.where(order[...] == p, fold_rows[p : p + 1, :], across)
    sub = lax.broadcasted_iota(jnp.int32, (cols, LANES), 0)
    lane = lax.broadcasted_iota(jnp.int32, (cols, LANES), 1)
    side = jnp.where(sub == 0, -1.0, jnp.where(sub == cols - 1, 1.0, 0.0))

    def beyond(c, index):
        at = pl.ds(c * tall + index, 1)
        return jnp.where(sub == 0, from_west[at, :], from_east[at, :])

    def folded_at(index):
        return pltpu.roll(across, LANES - 1 - index, 1)

    def copy(k):
        return pltpu.make_async_copy(out.at[:, k], out_hbm.at[:, k], sems.at[k])

    def level(k, carry):
        for c in range(chunks):
            part = slice(c * LANES, (c + 1) * LANES)
            sea, u, kap = sea_int[k, :, part].astype(F32), 0.25 * vel_u[k, :, part], 0.5 * kappa[k, :, part]
            mine = jnp.where(sub == 0, u - kap, u + kap)
            coef = side * sea * beyond(c, edge + levels + k) * (mine + beyond(c, edge + k))
            if c == chunks - 1:
                up = 0.25 * vel_v[k, :, part] + kap + folded_at(edge + k)
                fold = jnp.where(lane == LANES - 1, sea * folded_at(edge + levels + k) * up, 0.0)
            for a in range(count):
                x = lam[a, k, :, part]
                y = inner[a, k, :, part] + coef * (beyond(c, a * levels + k) - x)
                if c == chunks - 1:
                    y += fold * (folded_at(a * levels + k) - x)
                out[a, k, :, part] = y
        copy(k).start()
        return carry

    lax.fori_loop(0, levels, level, 0)
    for k in range(levels):
        copy(k).wait()


def cost(flops, count):
    return pl.CostEstimate(flops=0, bytes_accessed=0, transcendentals=0)


def body(lam, tracers, vel_u, vel_v, kappa, light, sea_int, partner, decay, w_in, w_out):
    count, levels, cols, rows = lam.shape
    reactions = w_in.shape[0]
    tall = (count + 2) * levels * (rows // LANES)
    n = lax.axis_size("space")
    params = pltpu.CompilerParams(vmem_limit_bytes=32 << 20)
    whole = jax.ShapeDtypeStruct(lam.shape, F32)
    shares = jax.ShapeDtypeStruct((2 * reactions, levels, cols, rows), F32)
    tile = jax.ShapeDtypeStruct((cols, LANES), F32)
    scalars = (w_in, w_out.T, decay, partner)
    arguments = (vel_u, vel_v, kappa, sea_int, lam, tracers, light)
    whole = jax.ShapeDtypeStruct(lam.shape, F32)
    vel_u, vel_v, kappa, sea_int, light, both, pack_east, pack_west, top, *spreads, to_tracers, fade, order = pl.pallas_call(
        pack_kernel,
        name="pack",
        out_shape=(
            *(jax.ShapeDtypeStruct(x.shape, x.dtype) for x in (vel_u, vel_v, kappa, sea_int, light)),
            jax.ShapeDtypeStruct((2, *lam.shape), F32),
            jax.ShapeDtypeStruct((tall + cols, LANES), F32),
            jax.ShapeDtypeStruct((tall + cols, LANES), F32),
            tile,
            *[jax.ShapeDtypeStruct((2 * reactions * cols, count * cols), BF16)] * 4,
            jax.ShapeDtypeStruct((2 * count * cols, reactions * cols), BF16),
            jax.ShapeDtypeStruct((count, rows), F32),
            jax.ShapeDtypeStruct((cols, LANES), jnp.int32),
        ),
        in_specs=[HBM] * 11,
        out_specs=(VMEM,) * 16,
        scratch_shapes=[*(pltpu.SMEM(x.shape, x.dtype) for x in scalars), pltpu.SemaphoreType.DMA((11,))],
        compiler_params=params,
        cost_estimate=cost(0, 4 * lam.size),
    )(*(pltpu.with_memory_space_constraint(x, pltpu.HBM) for x in scalars + arguments))
    eastward = [(s, (s + 1) % n) for s in range(n)]
    westward = [(s, (s - 1) % n) for s in range(n)]
    mirrored = [(s, n - 1 - s) for s in range(n)]
    from_fold = lax.ppermute(top, "space", [p for p in mirrored if p not in eastward + westward])
    from_east = lax.ppermute(pack_west, "space", westward)
    from_west = lax.ppermute(pack_east, "space", eastward)
    sums = pl.pallas_call(
        sums_kernel,
        name="sums",
        out_shape=shares,
        in_specs=[VMEM] * 3,
        out_specs=VMEM,
        compiler_params=params,
        cost_estimate=cost(32 * lam.size, 4 * lam.size),
    )(*spreads[:2], both)
    both_other = lax.ppermute(both, "tracer", [(0, 1), (1, 0)])
    inner = pl.pallas_call(
        inner_kernel,
        name="inner",
        out_shape=whole,
        in_specs=[VMEM] * 6,
        out_specs=VMEM,
        compiler_params=params,
        cost_estimate=cost(10 * lam.size, 4 * lam.size),
    )(fade, both, vel_u, vel_v, kappa, sea_int)
    inner = pl.pallas_call(
        react_kernel,
        name="react",
        out_shape=whole,
        in_specs=[VMEM] * 8,
        out_specs=VMEM,
        compiler_params=params,
        cost_estimate=cost(16 * lam.size, 4 * lam.size),
    )(*spreads[2:], to_tracers, light, sea_int, sums, both_other, inner)
    return pl.pallas_call(
        edges_kernel,
        name="edges",
        out_shape=whole,
        in_specs=[VMEM] * 10,
        out_specs=HBM,
        scratch_shapes=[
            pltpu.VMEM(lam.shape, F32),
            pltpu.SemaphoreType.DMA((levels,)),
        ],
        compiler_params=params,
        cost_estimate=cost(10 * lam.size, 4 * lam.size),
    )(order, both, vel_u, vel_v, kappa, sea_int, inner, from_west, from_east, from_fold)


def solution(mesh):
    placed = (
        P(("member", "tracer"), None, "space", None),
        P(("member", "tracer"), None, "space", None),
        P("member", "space", None),
        P("member", "space", None),
        P("member", "space", None),
        P("member", "space", None),
        P(None, "space", None),
        P("space"),
        P("tracer"),
        P(),
        P(),
    )
    return jax.shard_map(
        body,
        mesh=mesh,
        in_specs=placed,
        out_specs=P(("member", "tracer"), None, "space", None),
        check_vma=False,
    )
```

```python
import jax
import jax.numpy as jnp
from jax import lax
from jax.experimental import pallas as pl
from jax.experimental.pallas import tpu as pltpu
from jax.sharding import PartitionSpec as P

F32, BF16 = jnp.float32, jnp.bfloat16
VMEM = pl.BlockSpec(memory_space=pltpu.VMEM)
SMEM = pl.BlockSpec(memory_space=pltpu.SMEM)
HBM = pl.BlockSpec(memory_space=pltpu.HBM)
LANES = 128


def is_even():
    return lax.rem(lax.axis_index("space"), 2) == 0


def halves(x):
    high = x.astype(BF16)
    return high, (x - high.astype(F32)).astype(BF16)


def spread(target, weight, blocks, width, cols):
    lane = lax.broadcasted_iota(jnp.int32, (cols, width * cols), 1)
    sub = lax.broadcasted_iota(jnp.int32, (cols, width * cols), 0)
    square, diagonal = lane // cols, lane % cols == sub
    chosen = [square == other for other in range(width)]
    high, low = [], []
    for block in range(blocks):
        row = jnp.zeros((cols, width * cols), F32)
        for other in range(width):
            row = jnp.where(chosen[other], weight(block, other), row)
        row = jnp.where(diagonal, row, 0.0)
        top = row.astype(BF16).astype(F32)
        high.append(top)
        low.append(row - top)
    target[...] = jnp.concatenate(high + low, axis=0).astype(BF16)


def product(matrix, x):
    half = matrix.shape[0] // 2
    high, low = halves(x)
    first = jnp.dot(matrix[...], high, preferred_element_type=F32)
    return first[:half] + first[half:] + jnp.dot(matrix[:half], low, preferred_element_type=F32)


def pack_kernel(
    w_in_hbm, w_out_hbm, decay_hbm, partner_hbm, vel_u_hbm, vel_v_hbm, kappa_hbm, sea_hbm, lam_hbm, tracers_hbm, light_hbm,
    vel_u, vel_v, kappa, sea, light, both, pack_even, pack_odd, top_out, to_uptake, to_weighted, to_uptake_other, to_weighted_other, to_tracers, fade, order,
    w_in, w_out, decay, partner, sems,
):
    lam, tracers = both.at[0], both.at[1]
    count, levels, cols, rows = lam.shape
    edge = count * levels
    tall = edge + 2 * levels
    reactions = w_in.shape[0]
    sources = (w_in_hbm, w_out_hbm, decay_hbm, partner_hbm, vel_u_hbm, vel_v_hbm, kappa_hbm, sea_hbm, lam_hbm, tracers_hbm, light_hbm)
    targets = (w_in, w_out, decay, partner, vel_u, vel_v, kappa, sea, lam, tracers, light)
    copies = [pltpu.make_async_copy(s, t, sems.at[i]) for i, (s, t) in enumerate(zip(sources, targets))]
    for copy in copies:
        copy.start()
    first = lax.axis_index("tracer") * count
    for copy in copies[:4]:
        copy.wait()
    for a in range(count):
        fade[pl.ds(a, 1), :] = jnp.full((1, rows), decay[a], F32)
    sub = lax.broadcasted_iota(jnp.int32, (cols, LANES), 0)
    picks = jnp.zeros((cols, LANES), jnp.int32)
    for i in range(cols):
        picks = jnp.where(sub == i, lax.rem(partner[i], cols), picks)
    order[...] = picks
    spread(to_uptake, lambda h, a: w_in[h, first + a], reactions, count, cols)
    spread(to_weighted, lambda h, a: w_out[h, first + a], reactions, count, cols)
    second = count - first
    spread(to_uptake_other, lambda h, a: w_in[h, second + a], reactions, count, cols)
    spread(to_weighted_other, lambda h, a: w_out[h, second + a], reactions, count, cols)
    spread(to_tracers, lambda a, h: w_in[h, first + a], count, reactions, cols)
    for copy in copies[4:9]:
        copy.wait()

    even = is_even()
    for target, is_east in ((pack_even, even), (pack_odd, jnp.logical_not(even))):
        line = pl.ds(jnp.where(is_east, cols - 1, 0), 1)
        sign = jnp.where(is_east, -0.5, 0.5)

        def put(index, value):
            for c in range(rows // LANES):
                target[pl.ds(c * tall + index, 1), :] = value[:, c * LANES : (c + 1) * LANES]

        for a in range(count):
            for k in range(levels):
                put(a * levels + k, lam[a, k, line, :])
        for k in range(levels):
            put(edge + k, 0.25 * vel_u[k, line, :] + sign * kappa[k, line, :])
            put(edge + levels + k, sea[k, line, :].astype(F32))

    lane = lax.broadcasted_iota(jnp.int32, (cols, LANES), 1)
    top = jnp.zeros((cols, LANES), F32)
    last = rows - LANES

    def placed(top, index, value):
        return jnp.where(lane == index, pltpu.roll(value, index + 1, 1), top)

    for a in range(count):
        for k in range(levels):
            top = placed(top, a * levels + k, lam[a, k, :, last:])
    for k in range(levels):
        top = placed(top, edge + k, 0.5 * kappa[k, :, last:] - 0.25 * vel_v[k, :, last:])
        top = placed(top, edge + levels + k, sea[k, :, last:].astype(F32))
    for target in (pack_even, pack_odd):
        target[pl.ds(rows // LANES * tall, cols), :] = top
    top_out[...] = top
    for copy in copies[9:]:
        copy.wait()


def inner_kernel(fade, both, vel_u, vel_v, kappa, sea_int, out):
    lam = both.at[0]
    count, levels, cols, rows = lam.shape
    col = lax.broadcasted_iota(jnp.int32, (cols, rows), 0)
    row = lax.broadcasted_iota(jnp.int32, (cols, rows), 1)

    def level(k, carry):
        sea = sea_int[k].astype(F32)
        u, v, kap = 0.25 * vel_u[k], 0.25 * vel_v[k], 0.5 * kappa[k]
        east = jnp.where(col == cols - 1, 0.0, sea * pltpu.roll(sea, cols - 1, 0))
        north = jnp.where(row == rows - 1, 0.0, sea * pltpu.roll(sea, rows - 1, 1))
        p, q = u + kap, u - kap
        pn, qn = v + kap, v - kap
        c_e = east * (p + pltpu.roll(p, cols - 1, 0))
        c_w = pltpu.roll(east * (q + pltpu.roll(q, cols - 1, 0)), 1, 0)
        c_n = north * (pn + pltpu.roll(pn, rows - 1, 1))
        c_s = pltpu.roll(north * (qn + pltpu.roll(qn, rows - 1, 1)), 1, 1)
        own = sea + (c_w + c_s - c_e - c_n)
        for a in range(count):
            x = lam[a, k]
            y = (own - fade[pl.ds(a, 1), :] * sea) * x
            y += c_e * pltpu.roll(x, cols - 1, 0)
            y -= c_w * pltpu.roll(x, 1, 0)
            y += c_n * pltpu.roll(x, rows - 1, 1)
            y -= c_s * pltpu.roll(x, 1, 1)
            out[a, k] = y
        return carry

    lax.fori_loop(0, levels, level, 0)


def react_kernel(to_uptake, to_weighted, to_uptake_other, to_weighted_other, to_tracers, light, sea, both, other, inner, out):
    count, levels, cols, rows = inner.shape
    reactions = to_uptake.shape[0] // (2 * cols)

    def planes(field, k):
        return field[:, k].reshape(count * cols, rows)

    for k in range(levels):
        lit = light[k] * sea[k].astype(F32)
        uptake = product(to_uptake, planes(both.at[1], k)) + product(to_uptake_other, planes(other.at[1], k))
        weighted = product(to_weighted, planes(both.at[0], k)) + product(to_weighted_other, planes(other.at[0], k))
        gain = []
        for h in range(reactions):
            part = slice(h * cols, (h + 1) * cols)
            t = jnp.tanh(uptake[part])
            gain.append(lit * (1.0 - t * t) * weighted[part])
        coupled = product(to_tracers, jnp.concatenate(gain, axis=0))
        out[:, k] = inner[:, k] + coupled.reshape(count, cols, rows)


def mirrored_by_neighbour():
    place, strips = lax.axis_index("space"), lax.axis_size("space")
    neighbour = jnp.where(is_even(), lax.rem(place + strips - 1, strips), lax.rem(place + 1, strips))
    return neighbour == strips - 1 - place


def ordered(order, rows):
    across = jnp.zeros(rows.shape, F32)
    for p in range(rows.shape[0]):
        across = jnp.where(order[...] == p, rows[p : p + 1, :], across)
    return across


def folded_at(across, index):
    return pltpu.roll(across, LANES - 1 - index, 1)


def fold_coef(across, k, edge, levels, vel_v, kappa, sea_int):
    lane = lax.broadcasted_iota(jnp.int32, across.shape, 1)
    part = slice(kappa.shape[2] - LANES, kappa.shape[2])
    up = 0.25 * vel_v[k, :, part] + 0.5 * kappa[k, :, part] + folded_at(across, edge + k)
    sea = sea_int[k, :, part].astype(F32) * folded_at(across, edge + levels + k)
    return jnp.where(lane == LANES - 1, sea * up, 0.0)


def edges_kernel(
    order, both, vel_u, vel_v, kappa, sea_int, inner, from_even, from_odd, out_hbm, last, out, sems, last_sems
):
    lam = both.at[0]
    count, levels, cols, rows = lam.shape
    edge = count * levels
    tall = edge + 2 * levels
    chunks = rows // LANES
    folded = mirrored_by_neighbour()
    across = ordered(order, jnp.where(folded, from_odd[pl.ds(chunks * tall, cols), :], 0.0))
    sub = lax.broadcasted_iota(jnp.int32, (cols, LANES), 0)
    side = jnp.where(sub == 0, -1.0, jnp.where(sub == cols - 1, 1.0, 0.0))
    odd_row = jnp.logical_xor(sub == 0, jnp.logical_not(is_even()))

    def beyond(c, index):
        at = pl.ds(c * tall + index, 1)
        return jnp.where(odd_row, from_odd[at, :], from_even[at, :])

    def copy(k):
        return pltpu.make_async_copy(out.at[:, k], out_hbm.at[:, k, :, pl.ds(0, rows - LANES)], sems.at[k])

    def last_copy(k):
        return pltpu.make_async_copy(last.at[:, k], out_hbm.at[:, k, :, pl.ds(rows - LANES, LANES)], last_sems.at[k])

    def level(k, carry):
        for c in range(chunks):
            part = slice(c * LANES, (c + 1) * LANES)
            sea, u, kap = sea_int[k, :, part].astype(F32), 0.25 * vel_u[k, :, part], 0.5 * kappa[k, :, part]
            mine = jnp.where(sub == 0, u - kap, u + kap)
            coef = side * sea * beyond(c, edge + levels + k) * (mine + beyond(c, edge + k))
            if c == chunks - 1:
                fold = fold_coef(across, k, edge, levels, vel_v, kappa, sea_int)
            for a in range(count):
                x = lam[a, k, :, part]
                y = inner[a, k, :, part] + coef * (beyond(c, a * levels + k) - x)
                if c == chunks - 1:
                    last[a, k] = y + fold * (folded_at(across, a * levels + k) - x)
                else:
                    out[a, k, :, part] = y
        copy(k).start()

        @pl.when(folded)
        def _():
            last_copy(k).start()

        return carry

    lax.fori_loop(0, levels, level, 0)
    for k in range(levels):
        copy(k).wait()

    @pl.when(folded)
    def _():
        for k in range(levels):
            last_copy(k).wait()


def fold_kernel(result, order, both, vel_v, kappa, sea_int, last, from_fold, out_hbm, out, sem):
    lam = both.at[0]
    count, levels, cols, rows = lam.shape
    edge = count * levels

    @pl.when(jnp.logical_not(mirrored_by_neighbour()))
    def _():
        across = ordered(order, from_fold[...])
        for k in range(levels):
            fold = fold_coef(across, k, edge, levels, vel_v, kappa, sea_int)
            for a in range(count):
                x = lam[a, k, :, rows - LANES :]
                out[a, k] = last[a, k] + fold * (folded_at(across, a * levels + k) - x)
        copy = pltpu.make_async_copy(out, out_hbm.at[:, :, :, pl.ds(rows - LANES, LANES)], sem)
        copy.start()
        copy.wait()


def cost(flops, count):
    return pl.CostEstimate(flops=0, bytes_accessed=0, transcendentals=0)


def body(lam, tracers, vel_u, vel_v, kappa, light, sea_int, partner, decay, w_in, w_out):
    count, levels, cols, rows = lam.shape
    reactions = w_in.shape[0]
    tall = (count + 2) * levels * (rows // LANES)
    n = lax.axis_size("space")
    params = pltpu.CompilerParams(vmem_limit_bytes=32 << 20)
    whole = jax.ShapeDtypeStruct(lam.shape, F32)
    tile = jax.ShapeDtypeStruct((cols, LANES), F32)
    scalars = (w_in, w_out.T, decay, partner)
    arguments = (vel_u, vel_v, kappa, sea_int, lam, tracers, light)
    whole = jax.ShapeDtypeStruct(lam.shape, F32)
    vel_u, vel_v, kappa, sea_int, light, both, pack_even, pack_odd, top, *spreads, to_tracers, fade, order = pl.pallas_call(
        pack_kernel,
        name="pack",
        out_shape=(
            *(jax.ShapeDtypeStruct(x.shape, x.dtype) for x in (vel_u, vel_v, kappa, sea_int, light)),
            jax.ShapeDtypeStruct((2, *lam.shape), F32),
            jax.ShapeDtypeStruct((tall + cols, LANES), F32),
            jax.ShapeDtypeStruct((tall + cols, LANES), F32),
            tile,
            *[jax.ShapeDtypeStruct((2 * reactions * cols, count * cols), BF16)] * 4,
            jax.ShapeDtypeStruct((2 * count * cols, reactions * cols), BF16),
            jax.ShapeDtypeStruct((count, rows), F32),
            jax.ShapeDtypeStruct((cols, LANES), jnp.int32),
        ),
        in_specs=[HBM] * 11,
        out_specs=(VMEM,) * 16,
        scratch_shapes=[*(pltpu.SMEM(x.shape, x.dtype) for x in scalars), pltpu.SemaphoreType.DMA((11,))],
        compiler_params=params,
        cost_estimate=cost(0, 4 * lam.size),
    )(*(pltpu.with_memory_space_constraint(x, pltpu.HBM) for x in scalars + arguments))
    even_pairs = [(s, s ^ 1) for s in range(n)]
    odd_pairs = [(s, (s + 1) % n if s % 2 else (s - 1) % n) for s in range(n)]
    mirrored = [(s, n - 1 - s) for s in range(n)]
    from_fold = lax.ppermute(top, "space", [p for p in mirrored if p not in odd_pairs])
    from_even = lax.ppermute(pack_even, "space", even_pairs)
    from_odd = lax.ppermute(pack_odd, "space", odd_pairs)
    both_other = lax.ppermute(both, "tracer", [(0, 1), (1, 0)])
    inner = pl.pallas_call(
        inner_kernel,
        name="inner",
        out_shape=whole,
        in_specs=[VMEM] * 6,
        out_specs=VMEM,
        compiler_params=params,
        cost_estimate=cost(10 * lam.size, 4 * lam.size),
    )(fade, both, vel_u, vel_v, kappa, sea_int)
    inner = pl.pallas_call(
        react_kernel,
        name="react",
        out_shape=whole,
        in_specs=[VMEM] * 10,
        out_specs=VMEM,
        compiler_params=params,
        cost_estimate=cost(16 * lam.size, 4 * lam.size),
    )(*spreads, to_tracers, light, sea_int, both, both_other, inner)
    lanes = jax.ShapeDtypeStruct((count, levels, cols, LANES), F32)
    result, last = pl.pallas_call(
        edges_kernel,
        name="edges",
        out_shape=(whole, lanes),
        in_specs=[VMEM] * 9,
        out_specs=(HBM, VMEM),
        scratch_shapes=[
            pltpu.VMEM((count, levels, cols, rows - LANES), F32),
            pltpu.SemaphoreType.DMA((levels,)),
            pltpu.SemaphoreType.DMA((levels,)),
        ],
        compiler_params=params,
    )(order, both, vel_u, vel_v, kappa, sea_int, inner, from_even, from_odd)
    return pl.pallas_call(
        fold_kernel,
        name="fold",
        out_shape=whole,
        in_specs=[HBM] + [VMEM] * 7,
        out_specs=HBM,
        input_output_aliases={0: 0},
        scratch_shapes=[pltpu.VMEM(lanes.shape, F32), pltpu.SemaphoreType.DMA],
        compiler_params=params,
    )(pltpu.with_memory_space_constraint(result, pltpu.HBM), order, both, vel_v, kappa, sea_int, last, from_fold)


def solution(mesh):
    placed = (
        P(("member", "tracer"), None, "space", None),
        P(("member", "tracer"), None, "space", None),
        P("member", "space", None),
        P("member", "space", None),
        P("member", "space", None),
        P("member", "space", None),
        P(None, "space", None),
        P("space"),
        P("tracer"),
        P(),
        P(),
    )
    return jax.shard_map(
        body,
        mesh=mesh,
        in_specs=placed,
        out_specs=P(("member", "tracer"), None, "space", None),
        check_vma=False,
    )
```

```python
import jax
import jax.numpy as jnp
from jax import lax
from jax.experimental import pallas as pl
from jax.experimental.pallas import tpu as pltpu
from jax.sharding import PartitionSpec as P

F32, BF16 = jnp.float32, jnp.bfloat16
VMEM = pl.BlockSpec(memory_space=pltpu.VMEM)
SMEM = pl.BlockSpec(memory_space=pltpu.SMEM)
HBM = pl.BlockSpec(memory_space=pltpu.HBM)
LANES = 128


def is_even():
    return lax.rem(lax.axis_index("space"), 2) == 0


def halves(x):
    high = x.astype(BF16)
    return high, (x - high.astype(F32)).astype(BF16)


def spread(target, weights, start, cols):
    blocks, width = weights.shape[0], target.shape[1]
    lane = lax.broadcasted_iota(jnp.int32, weights.shape, 1)
    picked = jnp.take_along_axis(weights, lax.rem(start + lane // cols, LANES), axis=1)
    diagonal = (lane % cols == lax.broadcasted_iota(jnp.int32, weights.shape, 0))[:cols]
    rows = [jnp.where(diagonal, jnp.broadcast_to(picked[b : b + 1], (cols, LANES)), 0.0) for b in range(blocks)]
    whole = jnp.concatenate(rows, axis=0)
    high, low = halves(whole)
    half = blocks * cols
    target[:half] = high[:, :width]
    target[half:] = low[:, :width]
    return high, low


def product(matrix, x):
    half = matrix.shape[0] // 2
    high, low = halves(x)
    first = jnp.dot(matrix[...], high, preferred_element_type=F32)
    return first[:half] + first[half:] + jnp.dot(matrix[:half], low, preferred_element_type=F32)


def pack_kernel(
    w_in_hbm, w_out_hbm, decay_hbm, partner_hbm, vel_u_hbm, vel_v_hbm, kappa_hbm, sea_hbm, lam_hbm, tracers_hbm, light_hbm,
    vel_u, vel_v, kappa, sea, light, both, pack_even, pack_odd, top_out, to_uptake, to_weighted, to_uptake_other, to_weighted_other, to_tracers, fade, order,
    w_in, w_out, decay, partner, sems,
):
    lam, tracers = both.at[0], both.at[1]
    count, levels, cols, rows = lam.shape
    edge = count * levels
    tall = edge + 2 * levels
    reactions = w_in.shape[0]
    sources = (w_in_hbm, w_out_hbm, decay_hbm, partner_hbm, vel_u_hbm, vel_v_hbm, kappa_hbm, sea_hbm, lam_hbm, tracers_hbm, light_hbm)
    targets = (w_in, w_out, decay, partner, vel_u, vel_v, kappa, sea, lam, tracers, light)
    copies = [pltpu.make_async_copy(s, t, sems.at[i]) for i, (s, t) in enumerate(zip(sources, targets))]
    for i in (0, 1, 2, 3, 8, 4, 5, 6, 7, 9, 10):
        copies[i].start()
    first = lax.axis_index("tracer") * count
    for copy in copies[:4]:
        copy.wait()
    for a in range(count):
        fade[pl.ds(a, 1), :] = jnp.full((1, rows), decay[a], F32)
    sub = lax.broadcasted_iota(jnp.int32, (cols, LANES), 0)
    picks = jnp.zeros((cols, LANES), jnp.int32)
    for i in range(cols):
        picks = jnp.where(sub == i, lax.rem(partner[i], cols), picks)
    order[...] = picks
    second = count - first
    padding = jnp.zeros((reactions, LANES - w_in.shape[1]), F32)
    inward = jnp.concatenate([w_in[...], padding], axis=1)
    outward = jnp.concatenate([w_out[...], padding], axis=1)
    high, low = spread(to_uptake, inward, first, cols)
    spread(to_weighted, outward, first, cols)
    spread(to_uptake_other, inward, second, cols)
    spread(to_weighted_other, outward, second, cols)
    half = count * cols
    to_tracers[:half] = high.astype(F32).T[:half].astype(BF16)
    to_tracers[half:] = low.astype(F32).T[:half].astype(BF16)
    for copy in copies[4:9]:
        copy.wait()

    even = is_even()
    for target, is_east in ((pack_even, even), (pack_odd, jnp.logical_not(even))):
        line = pl.ds(jnp.where(is_east, cols - 1, 0), 1)
        sign = jnp.where(is_east, -0.5, 0.5)

        def put(index, value):
            for c in range(rows // LANES):
                target[pl.ds(c * tall + index, 1), :] = value[:, c * LANES : (c + 1) * LANES]

        for a in range(count):
            for k in range(levels):
                put(a * levels + k, lam[a, k, line, :])
        for k in range(levels):
            put(edge + k, 0.25 * vel_u[k, line, :] + sign * kappa[k, line, :])
            put(edge + levels + k, sea[k, line, :].astype(F32))

    lane = lax.broadcasted_iota(jnp.int32, (cols, LANES), 1)
    top = jnp.zeros((cols, LANES), F32)
    last = rows - LANES

    def placed(top, index, value):
        return jnp.where(lane == index, pltpu.roll(value, index + 1, 1), top)

    for a in range(count):
        for k in range(levels):
            top = placed(top, a * levels + k, lam[a, k, :, last:])
    for k in range(levels):
        top = placed(top, edge + k, 0.5 * kappa[k, :, last:] - 0.25 * vel_v[k, :, last:])
        top = placed(top, edge + levels + k, sea[k, :, last:].astype(F32))
    for target in (pack_even, pack_odd):
        target[pl.ds(rows // LANES * tall, cols), :] = top
    top_out[...] = top
    for copy in copies[9:]:
        copy.wait()


def inner_kernel(fade, both, vel_u, vel_v, kappa, sea_int, out):
    lam = both.at[0]
    count, levels, cols, rows = lam.shape
    col = lax.broadcasted_iota(jnp.int32, (cols, rows), 0)
    row = lax.broadcasted_iota(jnp.int32, (cols, rows), 1)

    def level(k, carry):
        sea = sea_int[k].astype(F32)
        u, v, kap = 0.25 * vel_u[k], 0.25 * vel_v[k], 0.5 * kappa[k]
        east = jnp.where(col == cols - 1, 0.0, sea * pltpu.roll(sea, cols - 1, 0))
        north = jnp.where(row == rows - 1, 0.0, sea * pltpu.roll(sea, rows - 1, 1))
        p, q = u + kap, u - kap
        pn, qn = v + kap, v - kap
        c_e = east * (p + pltpu.roll(p, cols - 1, 0))
        c_w = pltpu.roll(east * (q + pltpu.roll(q, cols - 1, 0)), 1, 0)
        c_n = north * (pn + pltpu.roll(pn, rows - 1, 1))
        c_s = pltpu.roll(north * (qn + pltpu.roll(qn, rows - 1, 1)), 1, 1)
        own = sea + (c_w + c_s - c_e - c_n)
        for a in range(count):
            x = lam[a, k]
            y = (own - fade[pl.ds(a, 1), :] * sea) * x
            y += c_e * pltpu.roll(x, cols - 1, 0)
            y -= c_w * pltpu.roll(x, 1, 0)
            y += c_n * pltpu.roll(x, rows - 1, 1)
            y -= c_s * pltpu.roll(x, 1, 1)
            out[a, k] = y
        return carry

    lax.fori_loop(0, levels, level, 0)


def react_kernel(to_uptake, to_weighted, to_uptake_other, to_weighted_other, to_tracers, light, sea, both, other, inner, out):
    count, levels, cols, rows = inner.shape
    reactions = to_uptake.shape[0] // (2 * cols)

    def planes(field, k):
        return field[:, k].reshape(count * cols, rows)

    for k in range(levels):
        lit = light[k] * sea[k].astype(F32)
        uptake = product(to_uptake, planes(both.at[1], k)) + product(to_uptake_other, planes(other.at[1], k))
        weighted = product(to_weighted, planes(both.at[0], k)) + product(to_weighted_other, planes(other.at[0], k))
        gain = []
        for h in range(reactions):
            part = slice(h * cols, (h + 1) * cols)
            t = jnp.tanh(uptake[part])
            gain.append(lit * (1.0 - t * t) * weighted[part])
        coupled = product(to_tracers, jnp.concatenate(gain, axis=0))
        out[:, k] = inner[:, k] + coupled.reshape(count, cols, rows)


def mirrored_by_neighbour():
    place, strips = lax.axis_index("space"), lax.axis_size("space")
    neighbour = jnp.where(is_even(), lax.rem(place + strips - 1, strips), lax.rem(place + 1, strips))
    return neighbour == strips - 1 - place


def ordered(order, rows):
    across = jnp.zeros(rows.shape, F32)
    for p in range(rows.shape[0]):
        across = jnp.where(order[...] == p, rows[p : p + 1, :], across)
    return across


def folded_at(across, index):
    return pltpu.roll(across, LANES - 1 - index, 1)


def fold_coef(across, k, edge, levels, vel_v, kappa, sea_int):
    lane = lax.broadcasted_iota(jnp.int32, across.shape, 1)
    part = slice(kappa.shape[2] - LANES, kappa.shape[2])
    up = 0.25 * vel_v[k, :, part] + 0.5 * kappa[k, :, part] + folded_at(across, edge + k)
    sea = sea_int[k, :, part].astype(F32) * folded_at(across, edge + levels + k)
    return jnp.where(lane == LANES - 1, sea * up, 0.0)


def edges_kernel(
    order, both, vel_u, vel_v, kappa, sea_int, inner, from_even, from_odd, out_hbm, last, out, sems, last_sems
):
    lam = both.at[0]
    count, levels, cols, rows = lam.shape
    edge = count * levels
    tall = edge + 2 * levels
    chunks = rows // LANES
    folded = mirrored_by_neighbour()
    across = ordered(order, jnp.where(folded, from_odd[pl.ds(chunks * tall, cols), :], 0.0))
    sub = lax.broadcasted_iota(jnp.int32, (cols, LANES), 0)
    side = jnp.where(sub == 0, -1.0, jnp.where(sub == cols - 1, 1.0, 0.0))
    odd_row = jnp.logical_xor(sub == 0, jnp.logical_not(is_even()))

    def beyond(c, index):
        at = pl.ds(c * tall + index, 1)
        return jnp.where(odd_row, from_odd[at, :], from_even[at, :])

    def copy(k):
        return pltpu.make_async_copy(out.at[:, k], out_hbm.at[:, k, :, pl.ds(0, rows - LANES)], sems.at[k])

    def last_copy(k):
        return pltpu.make_async_copy(last.at[:, k], out_hbm.at[:, k, :, pl.ds(rows - LANES, LANES)], last_sems.at[k])

    def level(k, carry):
        for c in range(chunks):
            part = slice(c * LANES, (c + 1) * LANES)
            sea, u, kap = sea_int[k, :, part].astype(F32), 0.25 * vel_u[k, :, part], 0.5 * kappa[k, :, part]
            mine = jnp.where(sub == 0, u - kap, u + kap)
            coef = side * sea * beyond(c, edge + levels + k) * (mine + beyond(c, edge + k))
            if c == chunks - 1:
                fold = fold_coef(across, k, edge, levels, vel_v, kappa, sea_int)
            for a in range(count):
                x = lam[a, k, :, part]
                y = inner[a, k, :, part] + coef * (beyond(c, a * levels + k) - x)
                if c == chunks - 1:
                    last[a, k] = y + fold * (folded_at(across, a * levels + k) - x)
                else:
                    out[a, k, :, part] = y
        copy(k).start()

        @pl.when(folded)
        def _():
            last_copy(k).start()

        return carry

    lax.fori_loop(0, levels, level, 0)
    for k in range(levels):
        copy(k).wait()

    @pl.when(folded)
    def _():
        for k in range(levels):
            last_copy(k).wait()


def fold_kernel(result, order, both, vel_v, kappa, sea_int, last, from_fold, out_hbm, out, sem):
    lam = both.at[0]
    count, levels, cols, rows = lam.shape
    edge = count * levels

    @pl.when(jnp.logical_not(mirrored_by_neighbour()))
    def _():
        across = ordered(order, from_fold[...])
        for k in range(levels):
            fold = fold_coef(across, k, edge, levels, vel_v, kappa, sea_int)
            for a in range(count):
                x = lam[a, k, :, rows - LANES :]
                out[a, k] = last[a, k] + fold * (folded_at(across, a * levels + k) - x)
        copy = pltpu.make_async_copy(out, out_hbm.at[:, :, :, pl.ds(rows - LANES, LANES)], sem)
        copy.start()
        copy.wait()


def cost(flops, count):
    return pl.CostEstimate(flops=0, bytes_accessed=0, transcendentals=0)


def body(lam, tracers, vel_u, vel_v, kappa, light, sea_int, partner, decay, w_in, w_out):
    count, levels, cols, rows = lam.shape
    reactions = w_in.shape[0]
    tall = (count + 2) * levels * (rows // LANES)
    n = lax.axis_size("space")
    params = pltpu.CompilerParams(vmem_limit_bytes=32 << 20)
    whole = jax.ShapeDtypeStruct(lam.shape, F32)
    tile = jax.ShapeDtypeStruct((cols, LANES), F32)
    scalars = (w_in, w_out.T, decay, partner)
    arguments = (vel_u, vel_v, kappa, sea_int, lam, tracers, light)
    whole = jax.ShapeDtypeStruct(lam.shape, F32)
    vel_u, vel_v, kappa, sea_int, light, both, pack_even, pack_odd, top, *spreads, to_tracers, fade, order = pl.pallas_call(
        pack_kernel,
        name="pack",
        out_shape=(
            *(jax.ShapeDtypeStruct(x.shape, x.dtype) for x in (vel_u, vel_v, kappa, sea_int, light)),
            jax.ShapeDtypeStruct((2, *lam.shape), F32),
            jax.ShapeDtypeStruct((tall + cols, LANES), F32),
            jax.ShapeDtypeStruct((tall + cols, LANES), F32),
            tile,
            *[jax.ShapeDtypeStruct((2 * reactions * cols, count * cols), BF16)] * 4,
            jax.ShapeDtypeStruct((2 * count * cols, reactions * cols), BF16),
            jax.ShapeDtypeStruct((count, rows), F32),
            jax.ShapeDtypeStruct((cols, LANES), jnp.int32),
        ),
        in_specs=[HBM] * 11,
        out_specs=(VMEM,) * 16,
        scratch_shapes=[*(pltpu.VMEM(x.shape, x.dtype) for x in scalars[:2]),
            *(pltpu.SMEM(x.shape, x.dtype) for x in scalars[2:]), pltpu.SemaphoreType.DMA((11,))],
        compiler_params=params,
        cost_estimate=cost(0, 4 * lam.size),
    )(*(pltpu.with_memory_space_constraint(x, pltpu.HBM) for x in scalars + arguments))
    even_pairs = [(s, s ^ 1) for s in range(n)]
    odd_pairs = [(s, (s + 1) % n if s % 2 else (s - 1) % n) for s in range(n)]
    mirrored = [(s, n - 1 - s) for s in range(n)]
    from_fold = lax.ppermute(top, "space", [p for p in mirrored if p not in odd_pairs])
    from_even = lax.ppermute(pack_even, "space", even_pairs)
    from_odd = lax.ppermute(pack_odd, "space", odd_pairs)
    both_other = lax.ppermute(both, "tracer", [(0, 1), (1, 0)])
    inner = pl.pallas_call(
        inner_kernel,
        name="inner",
        out_shape=whole,
        in_specs=[VMEM] * 6,
        out_specs=VMEM,
        compiler_params=params,
        cost_estimate=cost(10 * lam.size, 4 * lam.size),
    )(fade, both, vel_u, vel_v, kappa, sea_int)
    inner = pl.pallas_call(
        react_kernel,
        name="react",
        out_shape=whole,
        in_specs=[VMEM] * 10,
        out_specs=VMEM,
        compiler_params=params,
        cost_estimate=cost(16 * lam.size, 4 * lam.size),
    )(*spreads, to_tracers, light, sea_int, both, both_other, inner)
    lanes = jax.ShapeDtypeStruct((count, levels, cols, LANES), F32)
    result, last = pl.pallas_call(
        edges_kernel,
        name="edges",
        out_shape=(whole, lanes),
        in_specs=[VMEM] * 9,
        out_specs=(HBM, VMEM),
        scratch_shapes=[
            pltpu.VMEM((count, levels, cols, rows - LANES), F32),
            pltpu.SemaphoreType.DMA((levels,)),
            pltpu.SemaphoreType.DMA((levels,)),
        ],
        compiler_params=params,
    )(order, both, vel_u, vel_v, kappa, sea_int, inner, from_even, from_odd)
    return pl.pallas_call(
        fold_kernel,
        name="fold",
        out_shape=whole,
        in_specs=[HBM] + [VMEM] * 7,
        out_specs=HBM,
        input_output_aliases={0: 0},
        scratch_shapes=[pltpu.VMEM(lanes.shape, F32), pltpu.SemaphoreType.DMA],
        compiler_params=params,
    )(pltpu.with_memory_space_constraint(result, pltpu.HBM), order, both, vel_v, kappa, sea_int, last, from_fold)


def solution(mesh):
    placed = (
        P(("member", "tracer"), None, "space", None),
        P(("member", "tracer"), None, "space", None),
        P("member", "space", None),
        P("member", "space", None),
        P("member", "space", None),
        P("member", "space", None),
        P(None, "space", None),
        P("space"),
        P("tracer"),
        P(),
        P(),
    )
    return jax.shard_map(
        body,
        mesh=mesh,
        in_specs=placed,
        out_specs=P(("member", "tracer"), None, "space", None),
        check_vma=False,
    )
```
